32 devices in a mesh: gx: 2 (over core), gy: 4 (over y, x), gz: 4 (over z).
Axes of the slice: x: 2, y: 2, z: 4, core: 2. Of those that a mesh axis runs over, the one named last changes fastest.
Arguments:
- basis: bfloat16 [2, 4, 4, 96, 6144], P('gx', 'gy', 'gz'), may hold values from -0.078125 to 0.078125
- diagonal: float32 [2, 4, 4, 6144], P('gx', 'gy', 'gz'), may hold values from 0.05 to 1
- source: float32 [2, 4, 4, 16, 96], P('gx', 'gy', 'gz'), may hold values from -6 to 6
- well_cells: int32 [2, 4, 4, 16], P('gx', 'gy', 'gz'), may hold values from 0 to 95
Outputs:
- solution_field: float32 [2, 4, 4, 16, 3072], P('gx', 'gy', 'gz')
The draws below stay inside these ranges and needn't reach their ends.
All inputs are finite; a program needn't handle non-finite values.
Results may differ from the reference program's by a relative error of at most 0.0036.
Values sent between devices are 32-bit elements; how exact they have to be, the bound alone decides.
A program may use at most 64 MiB of HBM per device.

```python
import math
import jax
import jax.numpy as jnp
from jax import lax

MORTAR = 1024
MODES = 96
CASES = 16
ITERS = 2
N_GX = 2
N_GY = 4
N_GZ = 4


def with_ends(entries, own_key, least, top_value):
    longest = entries.shape.index(max(entries.shape))
    spots = []
    for shift in (0, 1):
        where = [jax.random.randint(jax.random.fold_in(own_key, axis), (), 0, length) for axis, length in enumerate(entries.shape)]
        where[longest] = (where[longest] + shift) % entries.shape[longest]
        spots.append(tuple(where))
    return entries.at[spots[0]].set(least).at[spots[1]].set(top_value)


def block_scale(rng, shape, split, smallest, largest):
    factor_of, own = 1.0, jax.random.fold_in(rng, 6)
    for position, shards_of in split:
        steps = jnp.exp(jax.random.uniform(jax.random.fold_in(own, position), (shards_of,), jnp.float32, smallest / len(split), largest / len(split)))
        factor_of = factor_of * jnp.repeat(steps, shape[position] // shards_of).reshape([-1 if axis == position else 1 for axis in range(len(shape))])
    return factor_of


def gaussian(rng, shape, spread, limit, pieces=(), held_as=jnp.bfloat16):
    entries = spread * jax.random.normal(rng, shape, jnp.float32)
    if pieces:
        entries = entries * block_scale(rng, shape, pieces, -0.22, 0.18)
    return jnp.clip(entries, -limit, limit).astype(held_as)


def setup_inputs(seed: int = 0) -> dict:
    splits = jax.random.split(jax.random.key(seed), 5)
    return {
        "basis": gaussian(splits[0], (N_GX, N_GY, N_GZ, MODES, 6 * MORTAR), (6 * MORTAR) ** -0.5, 0.078125, ((0, 2), (1, 4), (2, 4))),
        "diagonal": jnp.clip(jnp.exp(math.log(1.0) - 2.9957323 * jax.random.uniform(splits[1], (N_GX, N_GY, N_GZ, 6 * MORTAR), jnp.float32) ** block_scale(splits[1], (N_GX, N_GY, N_GZ, 6 * MORTAR), ((0, 2), (1, 4), (2, 4)), -0.2, 0.2)), 0.05, 1.0),
        "source": gaussian(splits[2], (N_GX, N_GY, N_GZ, CASES, MODES), 1.0, 6.0, ((0, 2), (1, 4), (2, 4)), jnp.float32),
        "well_cells": with_ends(jax.random.randint(splits[3], (N_GX, N_GY, N_GZ, CASES), 0, MODES), jax.random.fold_in(splits[3], 1), 0, MODES - 1).astype(jnp.int32),
    }


well_rate = 4.0


def shift_down(face_block, which_axis):
    length = face_block.shape[which_axis]
    kept_part = lax.slice_in_dim(face_block, 1, length, axis=which_axis)
    zero_part = jnp.zeros_like(lax.slice_in_dim(face_block, 0, 1, axis=which_axis))
    return jnp.concatenate([kept_part, zero_part], axis=which_axis)


def shift_up(face_block, which_axis):
    length = face_block.shape[which_axis]
    kept_part = lax.slice_in_dim(face_block, 0, length - 1, axis=which_axis)
    zero_part = jnp.zeros_like(lax.slice_in_dim(face_block, 0, 1, axis=which_axis))
    return jnp.concatenate([zero_part, kept_part], axis=which_axis)


def widen_field(owned_field):
    face_width = owned_field.shape[-1] // 3
    uppers = []
    for which_axis in range(3):
        lower_face = owned_field[..., which_axis * face_width:(which_axis + 1) * face_width]
        uppers.append(shift_down(lower_face, which_axis))
    return jnp.concatenate([owned_field] + uppers, axis=-1)


def assemble(responses):
    face_width = responses.shape[-1] // 6
    full_shape = responses.shape
    face_parts = []
    for which_axis in range(3):
        lower_face = responses[..., which_axis * face_width:(which_axis + 1) * face_width]
        upper_face = responses[..., (3 + which_axis) * face_width:(4 + which_axis) * face_width]
        summed = lower_face + shift_up(upper_face, which_axis)
        inside = lax.broadcasted_iota(jnp.int32, full_shape[:3] + (1, 1), which_axis) > 0
        face_parts.append(jnp.where(inside, summed, 0.0))
    return jnp.concatenate(face_parts, axis=-1)


def respond(local_field, basis, diagonal):
    leading = local_field.shape[:3]
    domain_count = leading[0] * leading[1] * leading[2]

    def one_domain(domain_items):
        basis_one, diag_one, vector = domain_items
        mode_values = lax.dot_general(vector.astype(jnp.bfloat16), basis_one, (((1,), (1,)), ((), ())), preferred_element_type=jnp.float32).astype(jnp.bfloat16)
        return diag_one * vector + jnp.dot(mode_values, basis_one, preferred_element_type=jnp.float32)

    flattened = lax.map(one_domain, (basis.reshape((domain_count,) + basis.shape[3:]), diagonal.reshape((domain_count,) + diagonal.shape[3:]), local_field.reshape((domain_count,) + local_field.shape[3:])))
    return flattened.reshape(local_field.shape)


def reference(basis, diagonal, source, well_cells):
    well_picks = lax.broadcasted_iota(jnp.int32, source.shape, 4) == well_cells[..., None].astype(jnp.int32)
    load_low = (source + well_rate * well_picks.astype(source.dtype)).astype(jnp.bfloat16)
    leading = source.shape[:3]
    domain_count = leading[0] * leading[1] * leading[2]

    def load_one(domain_items):
        basis_one, load_case = domain_items
        return jnp.dot(load_case, basis_one, preferred_element_type=jnp.float32)

    load_flux = lax.map(load_one, (basis.reshape((domain_count,) + basis.shape[3:]), load_low.reshape((domain_count,) + load_low.shape[3:])))
    load_flux = load_flux.reshape(leading + load_flux.shape[1:])
    right_side = assemble(load_flux)

    def operate(owned_field):
        return assemble(respond(widen_field(owned_field), basis, diagonal))

    def inner_sums(left_field, right_field):
        return jnp.sum(left_field * right_field, axis=(0, 1, 2, 4), keepdims=True)

    solution_field = jnp.zeros_like(right_side)
    residual = right_side
    direction = right_side
    norm_now = inner_sums(residual, residual)
    for iteration in range(ITERS):
        applied = operate(direction)
        step_size = norm_now / inner_sums(direction, applied)
        solution_field = solution_field + step_size * direction
        residual = residual - step_size * applied
        norm_next = inner_sums(residual, residual)
        direction = residual + (norm_next / norm_now) * direction
        norm_now = norm_next
    return solution_field
```

```python
import functools

import jax
import jax.numpy as jnp
from jax import lax
from jax.experimental import pallas as pl
from jax.experimental.pallas import tpu as pltpu
from jax.sharding import PartitionSpec as P

MESH = pl.DeviceIdType.MESH
AXES = ("gx", "gy", "gz")
WELL_RATE = 4.0
SEND_ORDER = (1, 4, 2, 5, 0, 3)
TAKE_ORDER = (0, 3, 2, 5, 1, 4)


def kernel(extents, basis_hbm, diag_ref, source_ref, wells_ref, out_ref,
           basis, flux, resp, got, sums, plane, column,
           load_sem, send_sem, recv_sem, plane_send, plane_recv, col_send, col_recv):
    width = basis.shape[1] // 6
    cases = source_ref.shape[0]
    at = tuple(lax.axis_index(a) for a in AXES)
    nx, ny, nz = extents

    def cut(face):
        return slice(face * width, (face + 1) * width)

    loads = {}
    for face in SEND_ORDER:
        loads[face] = pltpu.make_async_copy(
            basis_hbm.at[:, cut(face)], basis.at[:, cut(face)], load_sem.at[face])
        loads[face].start()

    plane_peers = []
    for k in range(1, nx * ny):
        kx, ky = k // ny, k % ny
        plane_peers.append((lax.rem(at[0] + kx, nx), lax.rem(at[1] + ky, ny), at[2]))
    col_peers = [(at[0], at[1], lax.rem(at[2] + k, nz)) for k in range(1, nz)]

    barrier = pltpu.get_barrier_semaphore()
    for peer in plane_peers + col_peers:
        pl.semaphore_signal(barrier, inc=1, device_id=peer, device_id_type=MESH)

    eye = (lax.broadcasted_iota(jnp.int32, (cases, cases), 0)
           == lax.broadcasted_iota(jnp.int32, (cases, cases), 1))
    cells = jnp.sum(jnp.where(eye, wells_ref[...].astype(jnp.float32), 0.0), axis=1, keepdims=True)
    modes = lax.broadcasted_iota(jnp.int32, source_ref.shape, 1).astype(jnp.float32)
    load_low = (source_ref[...] + jnp.where(modes == cells, WELL_RATE, 0.0)).astype(jnp.bfloat16)

    def has(face):
        axis = face % 3
        return at[axis] < extents[axis] - 1 if face >= 3 else at[axis] > 0

    def message(phase, face, source):
        axis, upper = face % 3, face >= 3
        target = list(at)
        target[axis] = at[axis] + (1 if upper else -1)
        landing = axis if upper else 3 + axis
        return pltpu.make_async_remote_copy(
            src_ref=source.at[:, cut(face)],
            dst_ref=got.at[phase, :, cut(landing)],
            send_sem=send_sem.at[phase, face],
            recv_sem=recv_sem.at[phase, landing],
            device_id=tuple(target), device_id_type=MESH)

    def arrival(phase, face):
        return pltpu.make_async_remote_copy(
            src_ref=flux.at[:, cut(face)],
            dst_ref=got.at[phase, :, cut(face)],
            send_sem=send_sem.at[phase, face],
            recv_sem=recv_sem.at[phase, face],
            device_id=tuple(at), device_id_type=MESH)

    def send(phase, face, source):
        @pl.when(has(face))
        def _():
            message(phase, face, source).start()

    def finish(phase, face, source):
        @pl.when(has(face))
        def _():
            message(phase, face, source).wait_send()

    for i, face in enumerate(SEND_ORDER):
        loads[face].wait()
        flux[:, cut(face)] = jnp.dot(load_low, basis[:, cut(face)], preferred_element_type=jnp.float32)
        if i == 0:
            pl.semaphore_wait(barrier, len(plane_peers) + len(col_peers))
        send(0, face, flux)

    def to_modes(field, face):
        return lax.dot_general(field.astype(jnp.bfloat16), basis[:, cut(face)],
                               (((1,), (1,)), ((), ())), preferred_element_type=jnp.float32)

    def taken(phase, face, source):
        arrived = has(face)

        @pl.when(arrived)
        def _():
            arrival(phase, face).wait_recv()

        return jnp.where(arrived, source[:, cut(face)] + got[phase, :, cut(face)], 0.0)

    def fold(x):
        return functools.reduce(jnp.add, [x[:, i:i + 128] for i in range(0, width, 128)])

    field = {}
    mode_values = jnp.zeros((cases, basis.shape[0]), jnp.float32)
    rr = jnp.zeros((cases, 128), jnp.float32)
    rw = jnp.zeros((cases, 128), jnp.float32)
    for face in TAKE_ORDER:
        f = taken(0, face, flux)
        field[face] = f
        mode_values = mode_values + to_modes(f, face)
        squares = f * f
        if face < 3:
            rr = rr + fold(squares)
        rw = rw + fold(diag_ref[:, cut(face)] * squares)
    m_low = mode_values.astype(jnp.bfloat16)

    for face in SEND_ORDER:
        resp[:, cut(face)] = diag_ref[:, cut(face)] * field[face] + jnp.dot(
            m_low, basis[:, cut(face)], preferred_element_type=jnp.float32)
        send(1, face, resp)

    def total(x):
        return jnp.sum(x, axis=1, keepdims=True)

    rr = total(rr)
    m_wide = m_low.astype(jnp.float32)
    rw = total(rw) + total(m_wide * mode_values)

    mode_values = jnp.zeros((cases, basis.shape[0]), jnp.float32)
    ww = jnp.zeros((cases, 128), jnp.float32)
    dw = jnp.zeros((cases, 128), jnp.float32)
    image = {}
    for face in TAKE_ORDER:
        f = taken(1, face, resp)
        if face < 3:
            image[face] = f
        mode_values = mode_values + to_modes(f, face)
        squares = f * f
        if face < 3:
            ww = ww + fold(squares)
        dw = dw + fold(diag_ref[:, cut(face)] * squares)
    ww = total(ww)
    m_wide = mode_values.astype(jnp.bfloat16).astype(jnp.float32)
    waw = total(dw) + total(m_wide * mode_values)

    half = cases // 2
    lane = lax.broadcasted_iota(jnp.int32, (half, 128), 1)
    packed = jnp.zeros((half, 128), jnp.float32)
    for k, value in enumerate((rr, rw, ww, waw)):
        packed = jnp.where(lane == 2 * k, value[:half], packed)
        packed = jnp.where(lane == 2 * k + 1, value[half:], packed)

    def everyone(step, value, peers, slots, s_sem, r_sem):
        sums[step] = value
        copies = []
        for k, peer in enumerate(peers):
            copies.append(pltpu.make_async_remote_copy(
                src_ref=sums.at[step], dst_ref=slots.at[k],
                send_sem=s_sem.at[k], recv_sem=r_sem.at[k],
                device_id=peer, device_id_type=MESH))
            copies[-1].start()
        for k, copy in enumerate(copies):
            copy.wait_recv()
            value = value + slots[k]
        return value, copies

    packed, copies0 = everyone(0, packed, plane_peers, plane, plane_send, plane_recv)
    packed, copies1 = everyone(1, packed, col_peers, column, col_send, col_recv)

    def value_of(k):
        return jnp.concatenate([packed[:, 2 * k:2 * k + 1], packed[:, 2 * k + 1:2 * k + 2]], axis=0)

    rr, rw, ww, waw = (value_of(k) for k in range(4))
    a0 = rr / rw
    norm1 = rr - 2.0 * a0 * rw + a0 * a0 * ww
    grow = 1.0 + norm1 / rr
    a1 = norm1 / (grow * grow * rw - 2.0 * grow * a0 * ww + a0 * a0 * waw)
    c_b = a0 + a1 * grow
    c_w = a0 * a1
    for face in range(3):
        out_ref[:, cut(face)] = c_b * field[face] - c_w * image[face]

    for face in SEND_ORDER:
        finish(0, face, flux)
        finish(1, face, resp)
    for copy in copies0 + copies1:
        copy.wait_send()


def solution(mesh):
    extents = tuple(mesh.shape[a] for a in AXES)

    def body(basis, diagonal, source, well_cells):
        modes, columns = basis.shape[-2:]
        cases = source.shape[-2]
        vmem = pl.BlockSpec(memory_space=pltpu.VMEM)
        dma = pltpu.SemaphoreType.DMA
        plane_count, col_count = extents[0] * extents[1] - 1, extents[2] - 1
        out = pl.pallas_call(
            functools.partial(kernel, extents),
            out_shape=jax.ShapeDtypeStruct((cases, columns // 2), jnp.float32),
            in_specs=[pl.BlockSpec(memory_space=pl.ANY), vmem, vmem, vmem],
            out_specs=vmem,
            scratch_shapes=[
                pltpu.VMEM((modes, columns), jnp.bfloat16),
                pltpu.VMEM((cases, columns), jnp.float32),
                pltpu.VMEM((cases, columns), jnp.float32),
                pltpu.VMEM((2, cases, columns), jnp.float32),
                pltpu.VMEM((2, cases // 2, 128), jnp.float32),
                pltpu.VMEM((plane_count, cases // 2, 128), jnp.float32),
                pltpu.VMEM((col_count, cases // 2, 128), jnp.float32),
                dma((6,)), dma((2, 6)), dma((2, 6)),
                dma((plane_count,)), dma((plane_count,)),
                dma((col_count,)), dma((col_count,)),
            ],
            compiler_params=pltpu.CompilerParams(
                collective_id=0, has_side_effects=True, vmem_limit_bytes=32 * 2**20),
        )(
            basis.reshape(modes, columns),
            diagonal.reshape(1, columns),
            source.reshape(cases, modes),
            well_cells.reshape(1, cases),
        )
        return out.reshape((1, 1, 1) + out.shape)

    in_specs = (
        P("gx", "gy", "gz", None, None),
        P("gx", "gy", "gz", None),
        P("gx", "gy", "gz", None, None),
        P("gx", "gy", "gz", None),
    )
    out_specs = P("gx", "gy", "gz", None, None)
    return jax.shard_map(body, mesh=mesh, in_specs=in_specs, out_specs=out_specs, check_vma=False)
```

```python
import functools

import jax
import jax.numpy as jnp
from jax import lax
from jax.experimental import pallas as pl
from jax.experimental.pallas import tpu as pltpu
from jax.sharding import PartitionSpec as P

MESH = pl.DeviceIdType.MESH
AXES = ("gx", "gy", "gz")
WELL_RATE = 4.0
SEND_ORDER = (1, 4, 2, 5, 0, 3)
TAKE_ORDER = (0, 3, 2, 5, 1, 4)


def kernel(extents, basis_hbm, diag_hbm, source_hbm, wells_hbm, out_ref,
           basis, diag_ref, source_ref, wells_ref, flux, resp, got, mine, theirs,
           load_sem, small_sem, send_sem, recv_sem, sum_send, sum_recv):
    width = basis.shape[1] // 6
    cases = source_ref.shape[0]
    at = tuple(lax.axis_index(a) for a in AXES)
    nx, ny, nz = extents

    def cut(face):
        return slice(face * width, (face + 1) * width)

    small = [pltpu.make_async_copy(a, b, small_sem.at[i]) for i, (a, b) in enumerate((
        (source_hbm, source_ref), (wells_hbm, wells_ref), (diag_hbm, diag_ref)))]
    small[0].start()
    small[1].start()
    loads = {}
    for face in SEND_ORDER:
        loads[face] = pltpu.make_async_copy(
            basis_hbm.at[:, cut(face)], basis.at[:, cut(face)], load_sem.at[face])
        loads[face].start()
    small[2].start()

    peers = []
    for k in reversed(range(1, nx * ny * nz)):
        kz, ky, kx = k // (nx * ny), k // nx % ny, k % nx
        peers.append((lax.rem(at[0] + kx, nx), lax.rem(at[1] + ky, ny), lax.rem(at[2] + kz, nz)))

    barrier = pltpu.get_barrier_semaphore()
    for peer in peers:
        pl.semaphore_signal(barrier, inc=1, device_id=peer, device_id_type=MESH)

    small[0].wait()
    small[1].wait()
    eye = (lax.broadcasted_iota(jnp.int32, (cases, cases), 0)
           == lax.broadcasted_iota(jnp.int32, (cases, cases), 1))
    cells = jnp.sum(jnp.where(eye, wells_ref[...].astype(jnp.float32), 0.0), axis=1, keepdims=True)
    modes = lax.broadcasted_iota(jnp.int32, source_ref.shape, 1).astype(jnp.float32)
    load_low = (source_ref[...] + jnp.where(modes == cells, WELL_RATE, 0.0)).astype(jnp.bfloat16)

    def has(face):
        axis = face % 3
        return at[axis] < extents[axis] - 1 if face >= 3 else at[axis] > 0

    def message(phase, face, source):
        axis, upper = face % 3, face >= 3
        target = list(at)
        target[axis] = at[axis] + (1 if upper else -1)
        landing = axis if upper else 3 + axis
        return pltpu.make_async_remote_copy(
            src_ref=source.at[:, cut(face)],
            dst_ref=got.at[phase, :, cut(landing)],
            send_sem=send_sem.at[phase, face],
            recv_sem=recv_sem.at[phase, landing],
            device_id=tuple(target), device_id_type=MESH)

    def arrival(phase, face):
        return pltpu.make_async_remote_copy(
            src_ref=flux.at[:, cut(face)],
            dst_ref=got.at[phase, :, cut(face)],
            send_sem=send_sem.at[phase, face],
            recv_sem=recv_sem.at[phase, face],
            device_id=tuple(at), device_id_type=MESH)

    def send(phase, face, source):
        @pl.when(has(face))
        def _():
            message(phase, face, source).start()

    def finish(phase, face, source):
        @pl.when(has(face))
        def _():
            message(phase, face, source).wait_send()

    for i, face in enumerate(SEND_ORDER):
        loads[face].wait()
        flux[:, cut(face)] = jnp.dot(load_low, basis[:, cut(face)], preferred_element_type=jnp.float32)
        if i == 0:
            pl.semaphore_wait(barrier, len(peers))
        send(0, face, flux)

    def to_modes(field, face):
        return lax.dot_general(field.astype(jnp.bfloat16), basis[:, cut(face)],
                               (((1,), (1,)), ((), ())), preferred_element_type=jnp.float32)

    def taken(phase, face, source):
        arrived = has(face)

        @pl.when(arrived)
        def _():
            arrival(phase, face).wait_recv()

        return jnp.where(arrived, source[:, cut(face)] + got[phase, :, cut(face)], 0.0)

    def fold(x):
        return functools.reduce(jnp.add, [x[:, i:i + 128] for i in range(0, width, 128)])

    small[2].wait()
    field = {}
    mode_values = jnp.zeros((cases, basis.shape[0]), jnp.float32)
    rr = jnp.zeros((cases, 128), jnp.float32)
    rw = jnp.zeros((cases, 128), jnp.float32)
    for face in TAKE_ORDER:
        f = taken(0, face, flux)
        field[face] = f
        mode_values = mode_values + to_modes(f, face)
        squares = f * f
        if face < 3:
            rr = rr + fold(squares)
        rw = rw + fold(diag_ref[:, cut(face)] * squares)
    m_low = mode_values.astype(jnp.bfloat16)

    for face in SEND_ORDER:
        resp[:, cut(face)] = diag_ref[:, cut(face)] * field[face] + jnp.dot(
            m_low, basis[:, cut(face)], preferred_element_type=jnp.float32)
        send(1, face, resp)

    def total(x):
        return jnp.sum(x, axis=1, keepdims=True)

    rr = total(rr)
    m_wide = m_low.astype(jnp.float32)
    rw = total(rw) + total(m_wide * mode_values)

    mode_values = jnp.zeros((cases, basis.shape[0]), jnp.float32)
    ww = jnp.zeros((cases, 128), jnp.float32)
    dw = jnp.zeros((cases, 128), jnp.float32)
    image = {}
    for face in TAKE_ORDER:
        f = taken(1, face, resp)
        if face < 3:
            image[face] = f
        mode_values = mode_values + to_modes(f, face)
        squares = f * f
        if face < 3:
            ww = ww + fold(squares)
        dw = dw + fold(diag_ref[:, cut(face)] * squares)
    ww = total(ww)
    m_wide = mode_values.astype(jnp.bfloat16).astype(jnp.float32)
    waw = total(dw) + total(m_wide * mode_values)

    lane = lax.broadcasted_iota(jnp.int32, (cases, 128), 1)
    row = lax.broadcasted_iota(jnp.int32, (cases, 128), 0)
    spread = jnp.zeros((cases, 128), jnp.float32)
    for k, value in enumerate((rr, rw, ww, waw)):
        spread = jnp.where(lane == row + k * cases, value, spread)
    mine[...] = jnp.sum(spread, axis=0, keepdims=True)
    copies = []
    for k, peer in enumerate(peers):
        copies.append(pltpu.make_async_remote_copy(
            src_ref=mine, dst_ref=theirs.at[k],
            send_sem=sum_send.at[k], recv_sem=sum_recv.at[k],
            device_id=peer, device_id_type=MESH))
        copies[-1].start()
    for copy in copies:
        copy.wait_recv()
    summed = mine[...] + jnp.sum(theirs[...], axis=0)

    def value_of(k):
        return total(jnp.where(lane == row + k * cases, summed, 0.0))

    rr, rw, ww, waw = (value_of(k) for k in range(4))
    a0 = rr / rw
    norm1 = rr - 2.0 * a0 * rw + a0 * a0 * ww
    grow = 1.0 + norm1 / rr
    a1 = norm1 / (grow * grow * rw - 2.0 * grow * a0 * ww + a0 * a0 * waw)
    c_b = a0 + a1 * grow
    c_w = a0 * a1
    for face in range(3):
        out_ref[:, cut(face)] = c_b * field[face] - c_w * image[face]

    for face in SEND_ORDER:
        finish(0, face, flux)
        finish(1, face, resp)
    for copy in copies:
        copy.wait_send()


def solution(mesh):
    extents = tuple(mesh.shape[a] for a in AXES)

    def body(basis, diagonal, source, well_cells):
        modes, columns = basis.shape[-2:]
        cases = source.shape[-2]
        vmem = pl.BlockSpec(memory_space=pltpu.VMEM)
        dma = pltpu.SemaphoreType.DMA
        others = extents[0] * extents[1] * extents[2] - 1
        out = pl.pallas_call(
            functools.partial(kernel, extents),
            out_shape=pltpu.VMEM((cases, columns // 2), jnp.float32),
            in_specs=[pl.BlockSpec(memory_space=pl.ANY)] * 4,
            out_specs=vmem,
            scratch_shapes=[
                pltpu.VMEM((modes, columns), jnp.bfloat16),
                pltpu.VMEM((1, columns), jnp.float32),
                pltpu.VMEM((cases, modes), jnp.float32),
                pltpu.VMEM((1, cases), jnp.int32),
                pltpu.VMEM((cases, columns), jnp.float32),
                pltpu.VMEM((cases, columns), jnp.float32),
                pltpu.VMEM((2, cases, columns), jnp.float32),
                pltpu.VMEM((1, 128), jnp.float32),
                pltpu.VMEM((others, 1, 128), jnp.float32),
                dma((6,)), dma((3,)), dma((2, 6)), dma((2, 6)),
                dma((others,)), dma((others,)),
            ],
            compiler_params=pltpu.CompilerParams(
                collective_id=0, has_side_effects=True, vmem_limit_bytes=60 * 2**20),
        )(
            basis.reshape(modes, columns),
            diagonal.reshape(1, columns),
            source.reshape(cases, modes),
            well_cells.reshape(1, cases),
        )
        return out.reshape((1, 1, 1) + out.shape)

    in_specs = (
        P("gx", "gy", "gz", None, None),
        P("gx", "gy", "gz", None),
        P("gx", "gy", "gz", None, None),
        P("gx", "gy", "gz", None),
    )
    out_specs = P("gx", "gy", "gz", None, None)
    return jax.shard_map(body, mesh=mesh, in_specs=in_specs, out_specs=out_specs, check_vma=False)
```

```python
import functools

import jax
import jax.numpy as jnp
from jax import lax
from jax.experimental import pallas as pl
from jax.experimental.pallas import tpu as pltpu
from jax.sharding import PartitionSpec as P

MESH = pl.DeviceIdType.MESH
AXES = ("gx", "gy", "gz")
WELL_RATE = 4.0
SEND_ORDER = (1, 4, 2, 5, 0, 3)
TAKE_ORDER = (0, 3, 2, 5, 1, 4)


def kernel(extents, basis_hbm, diag_hbm, source_hbm, wells_hbm, out_ref,
           basis, diag_ref, source_ref, wells_ref, flux, resp, got, mine, theirs,
           load_sem, small_sem, send_sem, recv_sem, sum_send, sum_recv, y_known, z_known):
    width = basis.shape[1] // 6
    cases = source_ref.shape[0]
    at = tuple(lax.axis_index(a) for a in AXES)
    nx, ny, nz = extents

    def cut(face):
        return slice(face * width, (face + 1) * width)

    small = [pltpu.make_async_copy(a, b, small_sem.at[i]) for i, (a, b) in enumerate((
        (source_hbm, source_ref), (wells_hbm, wells_ref), (diag_hbm, diag_ref)))]
    small[0].start()
    small[1].start()
    loads = {}
    for face in SEND_ORDER:
        loads[face] = pltpu.make_async_copy(
            basis_hbm.at[:, cut(face)], basis.at[:, cut(face)], load_sem.at[face])
        loads[face].start()
    small[2].start()

    peers = []
    for k in reversed(range(1, nx * ny * nz)):
        kz, ky, kx = k // (nx * ny), k // nx % ny, k % nx
        peers.append((lax.rem(at[0] + kx, nx), lax.rem(at[1] + ky, ny), lax.rem(at[2] + kz, nz)))

    x_peers = [(lax.rem(at[0] + k, nx), at[1], at[2]) for k in range(1, nx)]
    y_peers = [(at[0], lax.rem(at[1] + k, ny), at[2]) for k in range(1, ny)]
    z_peers = [(at[0], at[1], lax.rem(at[2] + k, nz)) for k in range(1, nz)]
    greeted = y_peers + z_peers + x_peers

    def tell(known, some):
        for peer in some:
            pl.semaphore_signal(known, inc=1, device_id=peer, device_id_type=MESH)

    barrier = pltpu.get_barrier_semaphore()
    for peer in greeted:
        pl.semaphore_signal(barrier, inc=1, device_id=peer, device_id_type=MESH)

    small[0].wait()
    small[1].wait()
    eye = (lax.broadcasted_iota(jnp.int32, (cases, cases), 0)
           == lax.broadcasted_iota(jnp.int32, (cases, cases), 1))
    cells = jnp.sum(jnp.where(eye, wells_ref[...].astype(jnp.float32), 0.0), axis=1, keepdims=True)
    modes = lax.broadcasted_iota(jnp.int32, source_ref.shape, 1).astype(jnp.float32)
    load_low = (source_ref[...] + jnp.where(modes == cells, WELL_RATE, 0.0)).astype(jnp.bfloat16)

    def has(face):
        axis = face % 3
        return at[axis] < extents[axis] - 1 if face >= 3 else at[axis] > 0

    def message(phase, face, source):
        axis, upper = face % 3, face >= 3
        target = list(at)
        target[axis] = at[axis] + (1 if upper else -1)
        landing = axis if upper else 3 + axis
        return pltpu.make_async_remote_copy(
            src_ref=source.at[:, cut(face)],
            dst_ref=got.at[phase, :, cut(landing)],
            send_sem=send_sem.at[phase, face],
            recv_sem=recv_sem.at[phase, landing],
            device_id=tuple(target), device_id_type=MESH)

    def arrival(phase, face):
        return pltpu.make_async_remote_copy(
            src_ref=flux.at[:, cut(face)],
            dst_ref=got.at[phase, :, cut(face)],
            send_sem=send_sem.at[phase, face],
            recv_sem=recv_sem.at[phase, face],
            device_id=tuple(at), device_id_type=MESH)

    def send(phase, face, source):
        @pl.when(has(face))
        def _():
            message(phase, face, source).start()

    def send_pair(phase, source):
        odd = lax.rem(at[1], 2) == 1

        @pl.when(odd)
        def _():
            send(phase, 4, source)
            send(phase, 1, source)

        @pl.when(jnp.logical_not(odd))
        def _():
            send(phase, 1, source)
            send(phase, 4, source)

    def finish(phase, face, source):
        @pl.when(has(face))
        def _():
            message(phase, face, source).wait_send()

    for i, face in enumerate(SEND_ORDER):
        loads[face].wait()
        flux[:, cut(face)] = jnp.dot(load_low, basis[:, cut(face)], preferred_element_type=jnp.float32)
        if i == 0:
            pl.semaphore_wait(barrier, len(greeted))
        if face == 4:
            send_pair(0, flux)
        elif face != 1:
            send(0, face, flux)

    tell(y_known, y_peers)

    def to_modes(field, face):
        return lax.dot_general(field.astype(jnp.bfloat16), basis[:, cut(face)],
                               (((1,), (1,)), ((), ())), preferred_element_type=jnp.float32)

    def taken(phase, face, source):
        arrived = has(face)

        @pl.when(arrived)
        def _():
            arrival(phase, face).wait_recv()

        return jnp.where(arrived, source[:, cut(face)] + got[phase, :, cut(face)], 0.0)

    def fold(x):
        return functools.reduce(jnp.add, [x[:, i:i + 128] for i in range(0, width, 128)])

    small[2].wait()
    field = {}
    mode_values = jnp.zeros((cases, basis.shape[0]), jnp.float32)
    rr = jnp.zeros((cases, 128), jnp.float32)
    rw = jnp.zeros((cases, 128), jnp.float32)
    for face in TAKE_ORDER:
        f = taken(0, face, flux)
        field[face] = f
        mode_values = mode_values + to_modes(f, face)
        squares = f * f
        if face < 3:
            rr = rr + fold(squares)
        rw = rw + fold(diag_ref[:, cut(face)] * squares)
    m_low = mode_values.astype(jnp.bfloat16)

    for face in SEND_ORDER:
        resp[:, cut(face)] = diag_ref[:, cut(face)] * field[face] + jnp.dot(
            m_low, basis[:, cut(face)], preferred_element_type=jnp.float32)
        if face == 4:
            send_pair(1, resp)
        elif face != 1:
            send(1, face, resp)

    pl.semaphore_wait(y_known, len(y_peers))
    tell(z_known, z_peers)

    def total(x):
        return jnp.sum(x, axis=1, keepdims=True)

    rr = total(rr)
    m_wide = m_low.astype(jnp.float32)
    rw = total(rw) + total(m_wide * mode_values)

    mode_values = jnp.zeros((cases, basis.shape[0]), jnp.float32)
    ww = jnp.zeros((cases, 128), jnp.float32)
    dw = jnp.zeros((cases, 128), jnp.float32)
    image = {}
    for face in TAKE_ORDER:
        f = taken(1, face, resp)
        if face < 3:
            image[face] = f
        mode_values = mode_values + to_modes(f, face)
        squares = f * f
        if face < 3:
            ww = ww + fold(squares)
        dw = dw + fold(diag_ref[:, cut(face)] * squares)
    ww = total(ww)
    m_wide = mode_values.astype(jnp.bfloat16).astype(jnp.float32)
    waw = total(dw) + total(m_wide * mode_values)

    lane = lax.broadcasted_iota(jnp.int32, (cases, 128), 1)
    row = lax.broadcasted_iota(jnp.int32, (cases, 128), 0)
    spread = jnp.zeros((cases, 128), jnp.float32)
    for k, value in enumerate((rr, rw, ww, waw)):
        spread = jnp.where(lane == row + k * cases, value, spread)
    mine[...] = jnp.sum(spread, axis=0, keepdims=True)
    pl.semaphore_wait(z_known, len(z_peers))
    copies = []
    for k, peer in enumerate(peers):
        copies.append(pltpu.make_async_remote_copy(
            src_ref=mine, dst_ref=theirs.at[k],
            send_sem=sum_send.at[k], recv_sem=sum_recv.at[k],
            device_id=peer, device_id_type=MESH))
        copies[-1].start()
    for copy in copies:
        copy.wait_recv()
    summed = mine[...] + jnp.sum(theirs[...], axis=0)

    def value_of(k):
        return total(jnp.where(lane == row + k * cases, summed, 0.0))

    rr, rw, ww, waw = (value_of(k) for k in range(4))
    a0 = rr / rw
    norm1 = rr - 2.0 * a0 * rw + a0 * a0 * ww
    grow = 1.0 + norm1 / rr
    a1 = norm1 / (grow * grow * rw - 2.0 * grow * a0 * ww + a0 * a0 * waw)
    c_b = a0 + a1 * grow
    c_w = a0 * a1
    for face in range(3):
        out_ref[:, cut(face)] = c_b * field[face] - c_w * image[face]

    for face in SEND_ORDER:
        finish(0, face, flux)
        finish(1, face, resp)
    for copy in copies:
        copy.wait_send()


def solution(mesh):
    extents = tuple(mesh.shape[a] for a in AXES)

    def body(basis, diagonal, source, well_cells):
        modes, columns = basis.shape[-2:]
        cases = source.shape[-2]
        vmem = pl.BlockSpec(memory_space=pltpu.VMEM)
        dma = pltpu.SemaphoreType.DMA
        others = extents[0] * extents[1] * extents[2] - 1
        out = pl.pallas_call(
            functools.partial(kernel, extents),
            out_shape=pltpu.VMEM((cases, columns // 2), jnp.float32),
            in_specs=[pl.BlockSpec(memory_space=pl.ANY)] * 4,
            out_specs=vmem,
            scratch_shapes=[
                pltpu.VMEM((modes, columns), jnp.bfloat16),
                pltpu.VMEM((1, columns), jnp.float32),
                pltpu.VMEM((cases, modes), jnp.float32),
                pltpu.VMEM((1, cases), jnp.int32),
                pltpu.VMEM((cases, columns), jnp.float32),
                pltpu.VMEM((cases, columns), jnp.float32),
                pltpu.VMEM((2, cases, columns), jnp.float32),
                pltpu.VMEM((1, 128), jnp.float32),
                pltpu.VMEM((others, 1, 128), jnp.float32),
                dma((6,)), dma((3,)), dma((2, 6)), dma((2, 6)),
                dma((others,)), dma((others,)),
                pltpu.SemaphoreType.REGULAR, pltpu.SemaphoreType.REGULAR,
            ],
            compiler_params=pltpu.CompilerParams(
                collective_id=0, has_side_effects=True, vmem_limit_bytes=60 * 2**20),
        )(
            basis.reshape(modes, columns),
            diagonal.reshape(1, columns),
            source.reshape(cases, modes),
            well_cells.reshape(1, cases),
        )
        return out.reshape((1, 1, 1) + out.shape)

    in_specs = (
        P("gx", "gy", "gz", None, None),
        P("gx", "gy", "gz", None),
        P("gx", "gy", "gz", None, None),
        P("gx", "gy", "gz", None),
    )
    out_specs = P("gx", "gy", "gz", None, None)
    return jax.shard_map(body, mesh=mesh, in_specs=in_specs, out_specs=out_specs, check_vma=False)
```

```python
import functools

import jax
import jax.numpy as jnp
from jax import lax
from jax.experimental import pallas as pl
from jax.experimental.pallas import tpu as pltpu
from jax.sharding import PartitionSpec as P

MESH = pl.DeviceIdType.MESH
AXES = ("gx", "gy", "gz")
WELL_RATE = 4.0
SEND_ORDER = (1, 4, 2, 5, 0, 3)
TAKE_ORDER = (0, 3, 2, 5, 1, 4)


def kernel(extents, basis_hbm, diag_hbm, source_hbm, wells_hbm, out_ref,
           basis, diag_ref, source_ref, wells_ref, flux, resp, got, mine, theirs,
           load_sem, small_sem, send_sem, recv_sem, sum_send, sum_recv, y_known, z_known):
    width = basis.shape[1] // 6
    cases = source_ref.shape[0]
    at = tuple(lax.axis_index(a) for a in AXES)
    nx, ny, nz = extents

    def cut(face):
        return slice(face * width, (face + 1) * width)

    small = [pltpu.make_async_copy(a, b, small_sem.at[i]) for i, (a, b) in enumerate((
        (source_hbm, source_ref), (wells_hbm, wells_ref), (diag_hbm, diag_ref)))]
    small[0].start()
    small[1].start()
    loads = {}
    for face in SEND_ORDER:
        loads[face] = pltpu.make_async_copy(
            basis_hbm.at[:, cut(face)], basis.at[:, cut(face)], load_sem.at[face])
        loads[face].start()
    small[2].start()

    peers = []
    for k in reversed(range(1, nx * ny * nz)):
        kz, ky, kx = k // (nx * ny), k // nx % ny, k % nx
        peers.append((lax.rem(at[0] + kx, nx), lax.rem(at[1] + ky, ny), lax.rem(at[2] + kz, nz)))

    x_peers = [(lax.rem(at[0] + k, nx), at[1], at[2]) for k in range(1, nx)]
    y_peers = [(at[0], lax.rem(at[1] + k, ny), at[2]) for k in range(1, ny)]
    z_peers = [(at[0], at[1], lax.rem(at[2] + k, nz)) for k in range(1, nz)]
    greeted = y_peers + z_peers + x_peers

    def tell(known, some):
        for peer in some:
            pl.semaphore_signal(known, inc=1, device_id=peer, device_id_type=MESH)

    barrier = pltpu.get_barrier_semaphore()
    for peer in greeted:
        pl.semaphore_signal(barrier, inc=1, device_id=peer, device_id_type=MESH)

    small[0].wait()
    small[1].wait()
    eye = (lax.broadcasted_iota(jnp.int32, (cases, cases), 0)
           == lax.broadcasted_iota(jnp.int32, (cases, cases), 1))
    cells = jnp.sum(jnp.where(eye, wells_ref[...].astype(jnp.float32), 0.0), axis=1, keepdims=True)
    modes = lax.broadcasted_iota(jnp.int32, source_ref.shape, 1).astype(jnp.float32)
    load_low = (source_ref[...] + jnp.where(modes == cells, WELL_RATE, 0.0)).astype(jnp.bfloat16)

    def has(face):
        axis = face % 3
        return at[axis] < extents[axis] - 1 if face >= 3 else at[axis] > 0

    def message(phase, face, source):
        axis, upper = face % 3, face >= 3
        target = list(at)
        target[axis] = at[axis] + (1 if upper else -1)
        landing = axis if upper else 3 + axis
        return pltpu.make_async_remote_copy(
            src_ref=source.at[:, cut(face)],
            dst_ref=got.at[phase, :, cut(landing)],
            send_sem=send_sem.at[phase, face],
            recv_sem=recv_sem.at[phase, landing],
            device_id=tuple(target), device_id_type=MESH)

    def arrival(phase, face):
        return pltpu.make_async_remote_copy(
            src_ref=flux.at[:, cut(face)],
            dst_ref=got.at[phase, :, cut(face)],
            send_sem=send_sem.at[phase, face],
            recv_sem=recv_sem.at[phase, face],
            device_id=tuple(at), device_id_type=MESH)

    def send(phase, face, source):
        @pl.when(has(face))
        def _():
            message(phase, face, source).start()

    def send_pair(phase, source):
        odd = lax.rem(at[1], 2) == 1

        @pl.when(odd)
        def _():
            send(phase, 4, source)
            send(phase, 1, source)

        @pl.when(jnp.logical_not(odd))
        def _():
            send(phase, 1, source)
            send(phase, 4, source)

    def finish(phase, face, source):
        @pl.when(has(face))
        def _():
            message(phase, face, source).wait_send()

    for i, face in enumerate(SEND_ORDER):
        loads[face].wait()
        flux[:, cut(face)] = jnp.dot(load_low, basis[:, cut(face)], preferred_element_type=jnp.float32)
        if i == 0:
            pl.semaphore_wait(barrier, len(greeted))
        if face == 4:
            send_pair(0, flux)
        elif face != 1:
            send(0, face, flux)

    tell(y_known, y_peers)

    def to_modes(field, face):
        return lax.dot_general(field.astype(jnp.bfloat16), basis[:, cut(face)],
                               (((1,), (1,)), ((), ())), preferred_element_type=jnp.float32)

    def taken(phase, face, source):
        arrived = has(face)

        @pl.when(arrived)
        def _():
            arrival(phase, face).wait_recv()

        return jnp.where(arrived, source[:, cut(face)] + got[phase, :, cut(face)], 0.0)

    def fold(x):
        return functools.reduce(jnp.add, [x[:, i:i + 128] for i in range(0, width, 128)])

    small[2].wait()
    field = {}
    mode_values = jnp.zeros((cases, basis.shape[0]), jnp.float32)
    rr = jnp.zeros((cases, 128), jnp.float32)
    rw = jnp.zeros((cases, 128), jnp.float32)
    for face in TAKE_ORDER:
        f = taken(0, face, flux)
        field[face] = f
        mode_values = mode_values + to_modes(f, face)
        squares = f * f
        if face < 3:
            rr = rr + fold(squares)
        rw = rw + fold(diag_ref[:, cut(face)] * squares)
    m_low = mode_values.astype(jnp.bfloat16)

    for face in SEND_ORDER:
        resp[:, cut(face)] = diag_ref[:, cut(face)] * field[face] + jnp.dot(
            m_low, basis[:, cut(face)], preferred_element_type=jnp.float32)
        if face == 4:
            send_pair(1, resp)
        elif face != 1:
            send(1, face, resp)

    pl.semaphore_wait(y_known, len(y_peers))
    tell(z_known, z_peers)

    def total(x):
        return jnp.sum(x, axis=1, keepdims=True)

    rr = total(rr)
    m_wide = m_low.astype(jnp.float32)
    rw = total(rw) + total(m_wide * mode_values)

    mode_values = jnp.zeros((cases, basis.shape[0]), jnp.float32)
    ww = jnp.zeros((cases, 128), jnp.float32)
    dw = jnp.zeros((cases, 128), jnp.float32)
    image = {}
    for face in TAKE_ORDER:
        f = taken(1, face, resp)
        if face < 3:
            image[face] = f
        mode_values = mode_values + to_modes(f, face)
        squares = f * f
        if face < 3:
            ww = ww + fold(squares)
        dw = dw + fold(diag_ref[:, cut(face)] * squares)
    ww = total(ww)
    m_wide = mode_values.astype(jnp.bfloat16).astype(jnp.float32)
    waw = total(dw) + total(m_wide * mode_values)

    lane = lax.broadcasted_iota(jnp.int32, (cases, 128), 1)
    row = lax.broadcasted_iota(jnp.int32, (cases, 128), 0)
    spread = jnp.zeros((cases, 128), jnp.float32)
    for k, value in enumerate((rr, rw, ww, waw)):
        spread = jnp.where(lane == row + k * cases, value, spread)
    mine[...] = jnp.sum(spread, axis=0, keepdims=True)
    pl.semaphore_wait(z_known, len(z_peers))
    for k, peer in enumerate(peers):
        pltpu.make_async_remote_copy(
            src_ref=mine, dst_ref=theirs.at[k],
            send_sem=sum_send, recv_sem=sum_recv,
            device_id=peer, device_id_type=MESH).start()
    for face in SEND_ORDER:
        finish(0, face, flux)
        finish(1, face, resp)
    pltpu.make_async_copy(theirs, theirs, sum_send).wait()
    pltpu.make_async_copy(theirs, theirs, sum_recv).wait()
    summed = mine[...] + jnp.sum(theirs[...], axis=0)

    def value_of(k):
        return total(jnp.where(lane == row + k * cases, summed, 0.0))

    rr, rw, ww, waw = (value_of(k) for k in range(4))
    a0 = rr / rw
    norm1 = rr - 2.0 * a0 * rw + a0 * a0 * ww
    grow = 1.0 + norm1 / rr
    a1 = norm1 / (grow * grow * rw - 2.0 * grow * a0 * ww + a0 * a0 * waw)
    c_b = a0 + a1 * grow
    c_w = a0 * a1
    for face in range(3):
        out_ref[:, cut(face)] = c_b * field[face] - c_w * image[face]


def solution(mesh):
    extents = tuple(mesh.shape[a] for a in AXES)

    def body(basis, diagonal, source, well_cells):
        modes, columns = basis.shape[-2:]
        cases = source.shape[-2]
        vmem = pl.BlockSpec(memory_space=pltpu.VMEM)
        dma = pltpu.SemaphoreType.DMA
        others = extents[0] * extents[1] * extents[2] - 1
        out = pl.pallas_call(
            functools.partial(kernel, extents),
            out_shape=pltpu.VMEM((cases, columns // 2), jnp.float32),
            in_specs=[pl.BlockSpec(memory_space=pl.ANY)] * 4,
            out_specs=vmem,
            scratch_shapes=[
                pltpu.VMEM((modes, columns), jnp.bfloat16),
                pltpu.VMEM((1, columns), jnp.float32),
                pltpu.VMEM((cases, modes), jnp.float32),
                pltpu.VMEM((1, cases), jnp.int32),
                pltpu.VMEM((cases, columns), jnp.float32),
                pltpu.VMEM((cases, columns), jnp.float32),
                pltpu.VMEM((2, cases, columns), jnp.float32),
                pltpu.VMEM((1, 128), jnp.float32),
                pltpu.VMEM((others, 1, 128), jnp.float32),
                dma((6,)), dma((3,)), dma((2, 6)), dma((2, 6)),
                dma, dma,
                pltpu.SemaphoreType.REGULAR, pltpu.SemaphoreType.REGULAR,
            ],
            compiler_params=pltpu.CompilerParams(
                collective_id=0, has_side_effects=True, vmem_limit_bytes=60 * 2**20),
        )(
            basis.reshape(modes, columns),
            diagonal.reshape(1, columns),
            source.reshape(cases, modes),
            well_cells.reshape(1, cases),
        )
        return out.reshape((1, 1, 1) + out.shape)

    in_specs = (
        P("gx", "gy", "gz", None, None),
        P("gx", "gy", "gz", None),
        P("gx", "gy", "gz", None, None),
        P("gx", "gy", "gz", None),
    )
    out_specs = P("gx", "gy", "gz", None, None)
    return jax.shard_map(body, mesh=mesh, in_specs=in_specs, out_specs=out_specs, check_vma=False)
```

```python
import functools

import jax
import jax.numpy as jnp
from jax import lax
from jax.experimental import pallas as pl
from jax.experimental.pallas import tpu as pltpu
from jax.sharding import PartitionSpec as P

MESH = pl.DeviceIdType.MESH
AXES = ("gx", "gy", "gz")
WELL_RATE = 4.0
SEND_ORDER = (1, 4, 2, 5, 0, 3)
TAKE_ORDER = (0, 3, 2, 5, 1, 4)


def kernel(extents, basis_hbm, diag_hbm, source_hbm, wells_hbm, out_ref,
           basis, turned, diag_ref, source_ref, wells_ref, flux, resp, got, mine, theirs,
           load_sem, small_sem, send_sem, recv_sem, sum_send, sum_recv, y_known, z_known):
    width = basis.shape[1] // 6
    cases = source_ref.shape[0]
    at = tuple(lax.axis_index(a) for a in AXES)
    nx, ny, nz = extents

    def cut(face):
        return slice(face * width, (face + 1) * width)

    peers = []
    for k in reversed(range(1, nx * ny * nz)):
        kz, ky, kx = k // (nx * ny), k // nx % ny, k % nx
        peers.append((lax.rem(at[0] + kx, nx), lax.rem(at[1] + ky, ny), lax.rem(at[2] + kz, nz)))

    x_peers = [(lax.rem(at[0] + k, nx), at[1], at[2]) for k in range(1, nx)]
    y_peers = [(at[0], lax.rem(at[1] + k, ny), at[2]) for k in range(1, ny)]
    z_peers = [(at[0], at[1], lax.rem(at[2] + k, nz)) for k in range(1, nz)]
    greeted = y_peers + z_peers + x_peers

    def tell(known, some):
        for peer in some:
            pl.semaphore_signal(known, inc=1, device_id=peer, device_id_type=MESH)

    barrier = pltpu.get_barrier_semaphore()
    for peer in greeted:
        pl.semaphore_signal(barrier, inc=1, device_id=peer, device_id_type=MESH)

    small = [pltpu.make_async_copy(a, b, small_sem.at[i]) for i, (a, b) in enumerate((
        (source_hbm, source_ref), (wells_hbm, wells_ref), (diag_hbm, diag_ref)))]
    small[0].start()
    small[1].start()
    loads = {}
    for face in SEND_ORDER:
        loads[face] = pltpu.make_async_copy(
            basis_hbm.at[:, cut(face)], basis.at[:, cut(face)], load_sem.at[face])
        loads[face].start()
    small[2].start()

    small[0].wait()
    small[1].wait()
    eye = (lax.broadcasted_iota(jnp.int32, (cases, cases), 0)
           == lax.broadcasted_iota(jnp.int32, (cases, cases), 1))
    cells = jnp.sum(jnp.where(eye, wells_ref[...].astype(jnp.float32), 0.0), axis=1, keepdims=True)
    modes = lax.broadcasted_iota(jnp.int32, source_ref.shape, 1).astype(jnp.float32)
    load_low = (source_ref[...] + jnp.where(modes == cells, WELL_RATE, 0.0)).astype(jnp.bfloat16)

    def has(face):
        axis = face % 3
        return at[axis] < extents[axis] - 1 if face >= 3 else at[axis] > 0

    def message(phase, face, source):
        axis, upper = face % 3, face >= 3
        target = list(at)
        target[axis] = at[axis] + (1 if upper else -1)
        landing = axis if upper else 3 + axis
        return pltpu.make_async_remote_copy(
            src_ref=source.at[:, cut(face)],
            dst_ref=got.at[phase, :, cut(landing)],
            send_sem=send_sem.at[phase, face],
            recv_sem=recv_sem.at[phase, landing],
            device_id=tuple(target), device_id_type=MESH)

    def arrival(phase, face):
        return pltpu.make_async_remote_copy(
            src_ref=flux.at[:, cut(face)],
            dst_ref=got.at[phase, :, cut(face)],
            send_sem=send_sem.at[phase, face],
            recv_sem=recv_sem.at[phase, face],
            device_id=tuple(at), device_id_type=MESH)

    def send(phase, face, source):
        @pl.when(has(face))
        def _():
            message(phase, face, source).start()

    def send_pair(phase, source):
        odd = lax.rem(at[1], 2) == 1

        @pl.when(odd)
        def _():
            send(phase, 4, source)
            send(phase, 1, source)

        @pl.when(jnp.logical_not(odd))
        def _():
            send(phase, 1, source)
            send(phase, 4, source)

    def finish(phase, face, source):
        @pl.when(has(face))
        def _():
            message(phase, face, source).wait_send()

    for i, face in enumerate(SEND_ORDER):
        loads[face].wait()
        turned[cut(face), :] = basis[:, cut(face)].T
        flux[:, cut(face)] = jnp.dot(load_low, basis[:, cut(face)], preferred_element_type=jnp.float32)
        if i == 0:
            pl.semaphore_wait(barrier, len(greeted))
        if face == 4:
            send_pair(0, flux)
        elif face != 1:
            send(0, face, flux)

    tell(y_known, y_peers)

    def to_modes(field, face):
        return jnp.dot(field.astype(jnp.bfloat16), turned[cut(face), :],
                       preferred_element_type=jnp.float32)

    def taken(phase, face, source):
        arrived = has(face)

        @pl.when(arrived)
        def _():
            arrival(phase, face).wait_recv()

        return jnp.where(arrived, source[:, cut(face)] + got[phase, :, cut(face)], 0.0)

    def fold(x):
        return functools.reduce(jnp.add, [x[:, i:i + 128] for i in range(0, width, 128)])

    small[2].wait()
    field = {}
    mode_values = jnp.zeros((cases, basis.shape[0]), jnp.float32)
    rr = jnp.zeros((cases, 128), jnp.float32)
    rw = jnp.zeros((cases, 128), jnp.float32)
    for face in TAKE_ORDER:
        f = taken(0, face, flux)
        field[face] = f
        mode_values = mode_values + to_modes(f, face)
        squares = f * f
        if face < 3:
            rr = rr + fold(squares)
        rw = rw + fold(diag_ref[:, cut(face)] * squares)
    m_low = mode_values.astype(jnp.bfloat16)

    for face in SEND_ORDER:
        resp[:, cut(face)] = diag_ref[:, cut(face)] * field[face] + jnp.dot(
            m_low, basis[:, cut(face)], preferred_element_type=jnp.float32)
        if face == 4:
            send_pair(1, resp)
        elif face != 1:
            send(1, face, resp)

    pl.semaphore_wait(y_known, len(y_peers))
    tell(z_known, z_peers)

    def total(x):
        return jnp.sum(x, axis=1, keepdims=True)

    rr = total(rr)
    m_wide = m_low.astype(jnp.float32)
    rw = total(rw) + total(m_wide * mode_values)

    mode_values = jnp.zeros((cases, basis.shape[0]), jnp.float32)
    ww = jnp.zeros((cases, 128), jnp.float32)
    dw = jnp.zeros((cases, 128), jnp.float32)
    image = {}
    for face in TAKE_ORDER:
        f = taken(1, face, resp)
        if face < 3:
            image[face] = f
        mode_values = mode_values + to_modes(f, face)
        squares = f * f
        if face < 3:
            ww = ww + fold(squares)
        dw = dw + fold(diag_ref[:, cut(face)] * squares)
    ww = total(ww)
    m_wide = mode_values.astype(jnp.bfloat16).astype(jnp.float32)
    waw = total(dw) + total(m_wide * mode_values)

    lane = lax.broadcasted_iota(jnp.int32, (cases, 128), 1)
    row = lax.broadcasted_iota(jnp.int32, (cases, 128), 0)
    spread = jnp.zeros((cases, 128), jnp.float32)
    for k, value in enumerate((rr, rw, ww, waw)):
        spread = jnp.where(lane == row + k * cases, value, spread)
    mine[...] = jnp.sum(spread, axis=0, keepdims=True)
    pl.semaphore_wait(z_known, len(z_peers))
    for k, peer in enumerate(peers):
        pltpu.make_async_remote_copy(
            src_ref=mine, dst_ref=theirs.at[k],
            send_sem=sum_send, recv_sem=sum_recv,
            device_id=peer, device_id_type=MESH).start()
    for face in SEND_ORDER:
        finish(0, face, flux)
        finish(1, face, resp)
    pltpu.make_async_copy(theirs, theirs, sum_send).wait()
    pltpu.make_async_copy(theirs, theirs, sum_recv).wait()
    summed = mine[...] + jnp.sum(theirs[...], axis=0)

    def value_of(k):
        return total(jnp.where(lane == row + k * cases, summed, 0.0))

    rr, rw, ww, waw = (value_of(k) for k in range(4))
    a0 = rr / rw
    norm1 = rr - 2.0 * a0 * rw + a0 * a0 * ww
    grow = 1.0 + norm1 / rr
    a1 = norm1 / (grow * grow * rw - 2.0 * grow * a0 * ww + a0 * a0 * waw)
    c_b = a0 + a1 * grow
    c_w = a0 * a1
    for face in range(3):
        out_ref[:, cut(face)] = c_b * field[face] - c_w * image[face]


def solution(mesh):
    extents = tuple(mesh.shape[a] for a in AXES)

    def body(basis, diagonal, source, well_cells):
        modes, columns = basis.shape[-2:]
        cases = source.shape[-2]
        vmem = pl.BlockSpec(memory_space=pltpu.VMEM)
        dma = pltpu.SemaphoreType.DMA
        others = extents[0] * extents[1] * extents[2] - 1
        out = pl.pallas_call(
            functools.partial(kernel, extents),
            out_shape=pltpu.VMEM((cases, columns // 2), jnp.float32),
            in_specs=[pl.BlockSpec(memory_space=pl.ANY)] * 4,
            out_specs=vmem,
            scratch_shapes=[
                pltpu.VMEM((modes, columns), jnp.bfloat16),
                pltpu.VMEM((columns, modes), jnp.bfloat16),
                pltpu.VMEM((1, columns), jnp.float32),
                pltpu.VMEM((cases, modes), jnp.float32),
                pltpu.VMEM((1, cases), jnp.int32),
                pltpu.VMEM((cases, columns), jnp.float32),
                pltpu.VMEM((cases, columns), jnp.float32),
                pltpu.VMEM((2, cases, columns), jnp.float32),
                pltpu.VMEM((1, 128), jnp.float32),
                pltpu.VMEM((others, 1, 128), jnp.float32),
                dma((6,)), dma((3,)), dma((2, 6)), dma((2, 6)),
                dma, dma,
                pltpu.SemaphoreType.REGULAR, pltpu.SemaphoreType.REGULAR,
            ],
            compiler_params=pltpu.CompilerParams(
                collective_id=0, has_side_effects=True, vmem_limit_bytes=60 * 2**20),
        )(
            basis.reshape(modes, columns),
            diagonal.reshape(1, columns),
            source.reshape(cases, modes),
            well_cells.reshape(1, cases),
        )
        return out.reshape((1, 1, 1) + out.shape)

    in_specs = (
        P("gx", "gy", "gz", None, None),
        P("gx", "gy", "gz", None),
        P("gx", "gy", "gz", None, None),
        P("gx", "gy", "gz", None),
    )
    out_specs = P("gx", "gy", "gz", None, None)
    return jax.shard_map(body, mesh=mesh, in_specs=in_specs, out_specs=out_specs, check_vma=False)
```
